512 devices in a mesh: tm: 16 (over x, z_hi), space: 32 (over z_lo, y, core).
Axes of the slice: x: 4, y: 8, z: 8 (z_hi: 4, z_lo: 2; z = z_hi * 2 + z_lo), core: 2. Of those that a mesh axis runs over, the one named last changes fastest.
Arguments:
- guesses: float32 [16, 256, 32, 128], P('tm', 'space'), may hold values from -6 to 6
- forcing: float32 [16, 256, 32, 128], P('tm', 'space'), may hold values from -6 to 6
- initial: float32 [256, 32, 128], P('space'), may hold values from -12 to 12
- kappa: float32 [256, 32, 128], P('space'), may hold values from 0.02 to 0.1
- velocity: float32 [3, 256, 32, 128], P(None, 'space'), may hold values from -0.2 to 0.2
Outputs:
- fine_states: float32 [64, 256, 32, 128], P('tm', 'space')
The draws below stay inside these ranges and needn't reach their ends.
All inputs are finite; a program needn't handle non-finite values.
Results may differ from the reference program's by a relative error of at most 0.00002.
Values sent between devices are 32-bit elements; how exact they have to be, the bound alone decides.
No kernel may reach another device: no remote copies, remote signals or barrier semaphores. Data moves between devices by JAX's collectives and lax.ppermute only.
A program may use at most 64 MiB of HBM per device.

```python
import math
import jax
import jax.numpy as jnp

NX = 128
NY = 32
M = 4
NZ = 256
NC = 16
NFINE = 64


def block_scale(stream_key, extent, cuts, least, largest):
    level, own = 1.0, jax.random.fold_in(stream_key, 6)
    for position, blocks in cuts:
        steps = jnp.exp(jax.random.uniform(jax.random.fold_in(own, position), (blocks,), jnp.float32, least / len(cuts), largest / len(cuts)))
        level = level * jnp.repeat(steps, extent[position] // blocks).reshape([-1 if axis == position else 1 for axis in range(len(extent))])
    return level


def scatter_about(rng, dims, scale, most, shards=(), held_as=jnp.bfloat16):
    entries = jax.random.normal(rng, dims, jnp.float32) * scale
    if len(shards) > 0:
        entries = block_scale(rng, dims, shards, -0.22, 0.18) * entries
    return jnp.clip(entries, min=-most, max=most).astype(held_as)


def setup_inputs(seed: int = 0) -> dict:
    splits = jax.random.split(jax.random.key(seed), 6)
    guesses = scatter_about(splits[0], (NC, NZ, NY, NX), 1.0, 6.0, ((0, 16), (1, 32)), jnp.float32)
    forcing = scatter_about(splits[1], (NC, NZ, NY, NX), 1.0, 6.0, ((0, 16), (1, 32)), jnp.float32)
    initial = scatter_about(splits[2], (NZ, NY, NX), 2.0, 12.0, ((0, 32),), jnp.float32)
    kappa = jnp.clip(jnp.exp(math.log(0.1) - 1.609438 * jax.random.uniform(splits[3], (NZ, NY, NX), jnp.float32) ** block_scale(splits[3], (NZ, NY, NX), ((0, 32),), -0.2, 0.2)), 0.02, 0.1)
    velocity = jnp.clip(jax.random.uniform(splits[4], (3, NZ, NY, NX), jnp.float32, -0.2, 0.2) * block_scale(splits[4], (3, NZ, NY, NX), ((1, 32),), -0.4, 0.0), -0.2, 0.2)
    return {"guesses": guesses, "forcing": forcing, "initial": initial, "kappa": kappa, "velocity": velocity}


step_size = 0.3


def advance(padded, diffuse, drift, source, delta):
    center = padded[..., 1:-1, :, :]
    margins = [(0, 0)] * (center.ndim - 2) + [(1, 1), (1, 1)]
    padded_xy = jnp.pad(center, margins)
    above_z = padded[..., 2:, :, :]
    below_z = padded[..., :-2, :, :]
    above_y = padded_xy[..., 2:, 1:-1]
    below_y = padded_xy[..., :-2, 1:-1]
    above_x = padded_xy[..., 1:-1, 2:]
    below_x = padded_xy[..., 1:-1, :-2]
    laplace = above_z + below_z + above_y + below_y + above_x + below_x - 6.0 * center
    transport = jnp.zeros_like(center)
    for speed, above, below in ((drift[0], above_z, below_z), (drift[1], above_y, below_y), (drift[2], above_x, below_x)):
        transport = transport + jnp.maximum(speed, 0.0) * (center - below) + jnp.minimum(speed, 0.0) * (above - center)
    return center + delta * (diffuse * laplace - transport + source)


def pad_depth(field):
    return jnp.pad(field, [(0, 0)] * (field.ndim - 3) + [(1, 1), (0, 0), (0, 0)])


def reference(guesses, forcing, initial, kappa, velocity):
    states = jnp.concatenate([initial[None], guesses[:-1]], axis=0)
    for section in range(M):
        states = advance(pad_depth(states), kappa, velocity, forcing, step_size)
    residual = states - guesses
    correction = jnp.zeros_like(initial)
    errors = []
    for interval in range(NC):
        for repeat in range(2):
            correction = advance(pad_depth(correction), kappa, velocity, 0.0, 2.0 * step_size)
        correction = correction + residual[interval]
        errors.append(correction)
    corrected = guesses + jnp.stack(errors)
    states = jnp.concatenate([initial[None], corrected[:-1]], axis=0)
    stored = []
    for section in range(M - 1):
        states = advance(pad_depth(states), kappa, velocity, forcing, step_size)
        stored.append(states)
    stored.append(corrected)
    return jnp.stack(stored, axis=1).reshape(NFINE, NZ, NY, NX)
```

```python
import functools

import jax
import jax.numpy as jnp
from jax import lax
from jax.experimental import pallas as pl
from jax.experimental.pallas import tpu as pltpu
from jax.sharding import PartitionSpec as P


L = 8
NY, NX = 32, 128
STEP = 0.3
FINE_HALO = 5
COARSE_HALO = 7
SENT = (4, 6, 5, FINE_HALO)
FIRST = SENT[0] + SENT[1] + SENT[2] + 4 * FINE_HALO
MORE = 4 * (COARSE_HALO - FINE_HALO)
VMEM = pltpu.VMEM


def call(kernel, outs, scratch=()):
    return pl.pallas_call(
        kernel,
        out_shape=[jax.ShapeDtypeStruct((n, NY, NX) if isinstance(n, int) else n + (NY, NX), jnp.float32) for n in outs],
        scratch_shapes=[VMEM((n, NY, NX), jnp.float32) for n in scratch],
        compiler_params=pltpu.CompilerParams(vmem_limit_bytes=40 << 20),
    )


def stencil(u, at, cur, prev, nxt, coef, k):
    return (
        coef[0, k] * nxt
        + coef[1, k] * prev
        + coef[2, k] * pltpu.roll(cur, NY - 1, 0)
        + coef[3, k] * pltpu.roll(cur, 1, 0)
        + coef[4, k] * pltpu.roll(cur, NX - 1, 1)
        + coef[5, k] * pltpu.roll(cur, 1, 1)
        + coef[6, k] * cur
    )


def sweep(u, base, coef, coef_base, lo, hi, after=None):
    prev, cur = u[lo - 1 + base], u[lo + base]
    for z in range(lo, hi):
        nxt = u[z + 1 + base]
        new = stencil(u, z, cur, prev, nxt, coef, z + coef_base)
        u[z + base] = new if after is None else after(z, cur, new)
        prev, cur = cur, nxt


def coarse_twice(u, base, coef, halo):
    sweep(u, base, coef, COARSE_HALO, 1 - halo, L + halo - 1)
    sweep(u, base, coef, COARSE_HALO, 2 - halo, L + halo - 2)


def ext(own, outer, inner, z, outer_at=0, inner_at=0, own_at=0):
    if z < 0:
        return outer[outer_at - 1 - z]
    if z >= L:
        return inner[inner_at + z - L]
    return own[own_at + z]


def write_coefs(out, index, diffuse, vz, vy, vx, h):
    row = lax.broadcasted_iota(jnp.int32, (NY, NX), 0)
    lane = lax.broadcasted_iota(jnp.int32, (NY, NX), 1)
    zero = jnp.zeros((NY, NX), jnp.float32)

    def pair(v):
        return h * (diffuse - jnp.minimum(v, 0.0)), h * (diffuse + jnp.maximum(v, 0.0))

    (above_z, below_z), (above_y, below_y), (above_x, below_x) = pair(vz), pair(vy), pair(vx)
    out[0, index] = above_z
    out[1, index] = below_z
    out[2, index] = jnp.where(row == NY - 1, zero, above_y)
    out[3, index] = jnp.where(row == 0, zero, below_y)
    out[4, index] = jnp.where(lane == NX - 1, zero, above_x)
    out[5, index] = jnp.where(lane == 0, zero, below_x)
    out[6, index] = 1.0 - (above_z + below_z + above_y + below_y + above_x + below_x)


def pack_kernel(guesses, forcing, initial, kappa, velocity, own, outer, inner, more_outer, more_inner):
    odd = lax.axis_index("space") % 2
    first = (lax.axis_index("tm") == 0).astype(jnp.float32)
    sign = (1 - 2 * odd).astype(jnp.float32)
    for z in range(L):
        i = z + odd * (L - 1 - 2 * z)
        own[z] = guesses[0, i]
        own[L + z] = first * initial[i]
        own[2 * L + z] = STEP * forcing[0, i]
        own[3 * L + z] = kappa[i]
        own[4 * L + z] = sign * velocity[0, i]
        own[5 * L + z] = velocity[1, i]
        own[6 * L + z] = velocity[2, i]
    at = 0
    for field in range(7):
        count = SENT[min(field, 3)]
        for i in range(count):
            outer[at + i] = own[field * L + i]
            inner[at + i] = own[field * L + L - 1 - i]
        at += count
    at = 0
    for field in range(3, 7):
        for i in range(FINE_HALO, COARSE_HALO):
            more_outer[at] = own[field * L + i]
            more_inner[at] = own[field * L + L - 1 - i]
            at += 1


def local_kernel(own, outer, inner, d, phi, coef, c, y, b):
    starts = (0, SENT[0], SENT[0] + SENT[1], SENT[0] + SENT[1] + SENT[2])

    def get(field, z):
        at = starts[min(field, 3)] + max(field - 3, 0) * FINE_HALO
        return ext(own, outer, inner, z, at, at, field * L)

    for z in range(-FINE_HALO, L + FINE_HALO):
        vz = get(4, z)
        if not 0 <= z < L:
            vz = -vz
        write_coefs(coef, z + FINE_HALO, get(3, z), vz, get(5, z), get(6, z), STEP)
    for z in range(-6, L + 6):
        y[z + 6] = get(1, z)
    for z in range(-4, L + 4):
        c[z + 4] = get(0, z)
    for step in range(4):
        halo = 5 - step
        sweep(y, 6, coef, FINE_HALO, -halo, L + halo, lambda z, cur, new: new + get(2, z))
        halo = 3 - step
        sweep(c, 4, coef, FINE_HALO, -halo, L + halo)
    for z in range(-2, L + 2):
        b[z + 2] = y[z + 6] - get(0, z)
    for z in range(L):
        phi[z] = y[z + 6]
    for halo in (1, 0):
        sweep(b, 2, coef, FINE_HALO, -halo, L + halo, lambda z, cur, new: 2.0 * new - cur)
    for z in range(L):
        d[z] = c[z + 4] + b[z + 2]


def coarse_kernel(own, outer, inner, more_outer, more_inner, coef):
    start = FIRST - 4 * FINE_HALO
    more = COARSE_HALO - FINE_HALO

    def get(k, z):
        beyond = -1 - z if z < 0 else z - L
        if beyond < FINE_HALO:
            return ext(own, outer, inner, z, start + k * FINE_HALO, start + k * FINE_HALO, (3 + k) * L)
        return (more_outer if z < 0 else more_inner)[k * more + beyond - FINE_HALO]

    for z in range(-COARSE_HALO, L + COARSE_HALO):
        vz = get(1, z)
        if not 0 <= z < L:
            vz = -vz
        write_coefs(coef, z + COARSE_HALO, get(0, z), vz, get(2, z), get(3, z), 2.0 * STEP)


def slab_pack_kernel(g, outer, inner):
    at = 0
    for k, count in enumerate((6, 4, 2)):
        for i in range(count):
            outer[at] = g[k, i]
            inner[at] = g[k, L - 1 - i]
            at += 1


def slab_kernel(g, outer, inner, coef, total, relay, prefix, v):
    place = lax.axis_index("tm") % 4
    for z in range(-6, L + 6):
        v[z + 6] = ext(g.at[0], outer, inner, z)

    def keep(wanted):
        @pl.when(place == wanted)
        def _():
            for z in range(-3, L + 3):
                prefix[z + 3] = v[z + 6]

    @pl.when(place < 2)
    def _():
        for z in range(L + 6):
            prefix[z] = jnp.zeros((NY, NX), jnp.float32)

    keep(2)
    coarse_twice(v, 6, coef, 6)
    for z in range(-4, L + 4):
        v[z + 6] += ext(g.at[1], outer, inner, z, 6, 6)
    keep(3)
    coarse_twice(v, 6, coef, 4)
    for z in range(-2, L + 2):
        v[z + 6] += ext(g.at[2], outer, inner, z, 10, 10)

    @pl.when(place == 0)
    def _():
        for z in range(L):
            relay[z] = v[z + 6]

    coarse_twice(v, 6, coef, 2)
    for z in range(L):
        total[z] = v[z + 6] + g[3, z]
        relay[L + z] = g[3, z]

    @pl.when(place > 0)
    def _():
        for z in range(L):
            relay[z] = total[z]


def chain1_kernel(far, far_outer, far_inner, middle, coef, outer, inner, u):
    place = lax.axis_index("tm") % 4
    for i in range(L):
        u[L - 1 - i] = far_outer[i]
        u[L + i] = far[i]
        u[2 * L + i] = far_inner[L - 1 - i]
    for i in range(4):
        if i < 3:

            @pl.when(place >= 3 - i)
            def _():
                coarse_twice(u, L, coef, 8 - 2 * i)
        else:
            coarse_twice(u, L, coef, 2)

    @pl.when(place == 3)
    def _():
        for z in range(L):
            u[L + z] += middle[z]

    for z in range(L):
        outer[z] = u[L + z]
        inner[z] = u[L + L - 1 - z]
    for i in range(6):
        outer[L + i] = middle[i]
        inner[L + i] = middle[L - 1 - i]


def chain2_kernel(held, outer, inner, middle, relay, shifted, own, coef, mine, to_outer, to_inner, u):
    place = lax.axis_index("tm") % 4
    first = (lax.axis_index("tm") == 0).astype(jnp.float32)
    for z in range(-L, 2 * L):
        u[L + z] = ext(held, outer, inner, z)
    for i in range(4):
        halo = 6 - 2 * i
        coarse_twice(u, L, coef, halo + 2)

        @pl.when(place == (2 - i) % 4)
        def _():
            for z in range(-halo, L + halo):
                u[L + z] += ext(relay, None, None, z) if i == 3 else ext(middle, outer, inner, z, L, L)

    for z in range(L):
        mine[z] = u[L + z]
        mine[L + z] = shifted[z] + own[L + z]
    for i in range(7):
        to_outer[i] = u[L + i]
        to_inner[i] = u[2 * L - 1 - i]
    for i in range(5):
        to_outer[7 + i] = relay[i]
        to_inner[7 + i] = relay[L - 1 - i]
    for i in range(3):
        to_outer[12 + i] = mine[L + i]
        to_inner[12 + i] = mine[2 * L - 1 - i]


def finish_kernel(mine, outer, inner, relay, prefix, g, phi, own, f_outer, f_inner, coef, fine, out, u, w):
    place = lax.axis_index("tm") % 4
    odd = lax.axis_index("space") % 2
    for z in range(-7, L + 7):
        u[7 + z] = ext(mine, outer, inner, z)

    def add_relay(halo):
        for z in range(-halo, L + halo):
            u[7 + z] += ext(relay, outer, inner, z, 7, 7)

    sweep(u, 7, coef, COARSE_HALO, -6, L + 6)
    sweep(u, 7, coef, COARSE_HALO, -5, L + 5)

    @pl.when(place == 2)
    def _():
        add_relay(5)

    sweep(u, 7, coef, COARSE_HALO, -4, L + 4)
    sweep(u, 7, coef, COARSE_HALO, -3, L + 3)

    @pl.when(place < 2)
    def _():
        add_relay(3)

    for z in range(-3, L + 3):
        g_t = u[7 + z] + prefix[3 + z]
        w[3 + z] = g_t
        u[7 + z] = g_t + ext(mine, outer, inner, z, 12, 12, L)
    coarse_twice(w, 3, coef, 2)

    @pl.when(place == 0)
    def _():
        for z in range(L):
            out[3, z + odd * (L - 1 - 2 * z)] = w[3 + z] + phi[z] + relay[L + z]

    @pl.when(place > 0)
    def _():
        for z in range(L):
            out[3, z + odd * (L - 1 - 2 * z)] = w[3 + z] + phi[z] + g[place - 1, z]

    at = SENT[0] + SENT[1]
    for step in range(3):
        halo = 2 - step
        sweep(u, 7, fine, FINE_HALO, -halo, L + halo,
              lambda z, cur, new: new + ext(own, f_outer, f_inner, z, at, at, 2 * L))
        for z in range(L):
            out[step, z + odd * (L - 1 - 2 * z)] = u[7 + z]


def body(guesses, forcing, initial, kappa, velocity):
    count, times = lax.axis_size("space"), lax.axis_size("tm")
    facing = [(i, i + 1) for i in range(1, count - 1, 2)]
    facing += [(b, a) for a, b in facing]
    paired = [(i, i ^ 1) for i in range(count)]

    def from_outer(x):
        return lax.ppermute(x, "space", facing)

    def from_inner(x):
        return lax.ppermute(x, "space", paired)

    def later(x, steps, moves=None):
        moves = [(i, i) for i in range(count)] if moves is None else moves
        pairs = [(t * count + a, (t + steps) * count + b) for t in range(times - steps) for a, b in moves]
        return lax.ppermute(x, ("tm", "space"), pairs)

    own, outer, inner, more_outer, more_inner = call(pack_kernel, (7 * L, FIRST, FIRST, MORE, MORE))(
        guesses, forcing, initial, kappa, velocity
    )
    outer, inner = from_outer(outer), from_inner(inner)
    more_outer, more_inner = from_outer(more_outer), from_inner(more_inner)
    d, phi, fine = call(local_kernel, (L, L, (7, L + 2 * FINE_HALO)), (L + 8, L + 12, L + 4))(own, outer, inner)
    (coef,) = call(coarse_kernel, ((7, L + 2 * COARSE_HALO),))(own, outer, inner, more_outer, more_inner)
    groups = [[4 * a + b for b in range(4)] for a in range(times // 4)]
    g = lax.all_gather(d, "tm", axis_index_groups=groups)
    shifted = later(phi, 1)
    slab_outer, slab_inner = call(slab_pack_kernel, (12, 12))(g)
    slab_outer, slab_inner = from_outer(slab_outer), from_inner(slab_inner)
    total, relay, prefix = call(slab_kernel, (L, 2 * L, L + 6), (L + 12,))(g, slab_outer, slab_inner, coef)
    far = later(total, 12)
    far_outer = later(total, 12, facing)
    far_inner = later(total, 12, paired)
    middle = later(total, 8)
    relay = later(relay, 4)
    c1_outer, c1_inner = call(chain1_kernel, (L + 6, L + 6), (3 * L,))(far, far_outer, far_inner, middle, coef)
    mine, c2_outer, c2_inner = call(chain2_kernel, (2 * L, 15, 15), (3 * L,))(
        c1_outer, from_outer(c1_outer), from_inner(c1_inner), middle, relay, shifted, own, coef
    )
    (out,) = call(finish_kernel, ((4, L),), (L + 14, L + 6))(
        mine, from_outer(c2_outer), from_inner(c2_inner), relay, prefix, g, phi, own, outer, inner, coef, fine
    )
    return out


def solution(mesh):
    placed = (
        P("tm", "space", None, None),
        P("tm", "space", None, None),
        P("space", None, None),
        P("space", None, None),
        P(None, "space", None, None),
    )
    return jax.shard_map(
        body, mesh=mesh, in_specs=placed, out_specs=P("tm", "space", None, None), check_vma=False
    )
```

```python
import functools

import jax
import jax.numpy as jnp
from jax import lax
from jax.experimental import pallas as pl
from jax.experimental.pallas import tpu as pltpu
from jax.sharding import PartitionSpec as P


L = 8
NY, NX = 32, 128
STEP = 0.3
FINE_HALO = 5
COARSE_HALO = 7
SENT = (4, 6, 5, COARSE_HALO)
FIRST = SENT[0] + SENT[1] + SENT[2] + 4 * COARSE_HALO
VMEM = pltpu.VMEM


def call(kernel, outs, scratch=()):
    return pl.pallas_call(
        kernel,
        out_shape=[jax.ShapeDtypeStruct((n, NY, NX) if isinstance(n, int) else n + (NY, NX), jnp.float32) for n in outs],
        scratch_shapes=[VMEM((n, NY, NX), jnp.float32) for n in scratch],
        compiler_params=pltpu.CompilerParams(vmem_limit_bytes=40 << 20),
    )


def stencil(u, at, cur, prev, nxt, coef, k):
    return (
        coef[0, k] * nxt
        + coef[1, k] * prev
        + coef[2, k] * pltpu.roll(cur, NY - 1, 0)
        + coef[3, k] * pltpu.roll(cur, 1, 0)
        + coef[4, k] * pltpu.roll(cur, NX - 1, 1)
        + coef[5, k] * pltpu.roll(cur, 1, 1)
        + coef[6, k] * cur
    )


def sweep(u, base, coef, coef_base, lo, hi, after=None):
    prev, cur = u[lo - 1 + base], u[lo + base]
    for z in range(lo, hi):
        nxt = u[z + 1 + base]
        new = stencil(u, z, cur, prev, nxt, coef, z + coef_base)
        u[z + base] = new if after is None else after(z, cur, new)
        prev, cur = cur, nxt


def coarse_twice(u, base, coef, halo):
    sweep(u, base, coef, COARSE_HALO, 1 - halo, L + halo - 1)
    sweep(u, base, coef, COARSE_HALO, 2 - halo, L + halo - 2)


def ext(own, outer, inner, z, outer_at=0, inner_at=0, own_at=0):
    if z < 0:
        return outer[outer_at - 1 - z]
    if z >= L:
        return inner[inner_at + z - L]
    return own[own_at + z]


def write_coefs(out, index, diffuse, vz, vy, vx, h):
    row = lax.broadcasted_iota(jnp.int32, (NY, NX), 0)
    lane = lax.broadcasted_iota(jnp.int32, (NY, NX), 1)
    zero = jnp.zeros((NY, NX), jnp.float32)

    def pair(v):
        return h * (diffuse - jnp.minimum(v, 0.0)), h * (diffuse + jnp.maximum(v, 0.0))

    (above_z, below_z), (above_y, below_y), (above_x, below_x) = pair(vz), pair(vy), pair(vx)
    out[0, index] = above_z
    out[1, index] = below_z
    out[2, index] = jnp.where(row == NY - 1, zero, above_y)
    out[3, index] = jnp.where(row == 0, zero, below_y)
    out[4, index] = jnp.where(lane == NX - 1, zero, above_x)
    out[5, index] = jnp.where(lane == 0, zero, below_x)
    out[6, index] = 1.0 - (above_z + below_z + above_y + below_y + above_x + below_x)


def pack_kernel(guesses, forcing, initial, kappa, velocity, own, outer, inner, held, sems):
    odd = lax.axis_index("space") % 2
    first = (lax.axis_index("tm") == 0).astype(jnp.float32)
    sign = (1 - 2 * odd).astype(jnp.float32)
    sources = (guesses.at[0], initial, forcing.at[0], kappa, velocity.at[0], velocity.at[1], velocity.at[2])
    copies = [pltpu.make_async_copy(source, held.at[k], sems.at[k]) for k, source in enumerate(sources)]
    for copy in copies:
        copy.start()
    at = 0
    for field, copy in enumerate(copies):
        copy.wait()
        for z in range(L):
            value = held[field, z + odd * (L - 1 - 2 * z)]
            if field in (1, 2, 4):
                value = (None, first, STEP, None, sign)[field] * value
            own[field * L + z] = value
        count = SENT[min(field, 3)]
        for i in range(count):
            outer[at + i] = own[field * L + i]
            inner[at + i] = own[field * L + L - 1 - i]
        at += count


def settle_kernel(held, own):
    for i in range(7 * L):
        own[i] = held[i]


def local_kernel(own, outer, inner, d, phi, coef, c, y, b):
    starts = (0, SENT[0], SENT[0] + SENT[1], SENT[0] + SENT[1] + SENT[2])

    def get(field, z):
        at = starts[min(field, 3)] + max(field - 3, 0) * COARSE_HALO
        return ext(own, outer, inner, z, at, at, field * L)

    for z in range(-FINE_HALO, L + FINE_HALO):
        vz = get(4, z)
        if not 0 <= z < L:
            vz = -vz
        write_coefs(coef, z + FINE_HALO, get(3, z), vz, get(5, z), get(6, z), STEP)
    for z in range(-6, L + 6):
        y[z + 6] = get(1, z)
    for z in range(-4, L + 4):
        c[z + 4] = get(0, z)
    for step in range(4):
        halo = 5 - step
        sweep(y, 6, coef, FINE_HALO, -halo, L + halo, lambda z, cur, new: new + get(2, z))
        halo = 3 - step
        sweep(c, 4, coef, FINE_HALO, -halo, L + halo)
    for z in range(-2, L + 2):
        b[z + 2] = y[z + 6] - get(0, z)
    for z in range(L):
        phi[z] = y[z + 6]
    for halo in (1, 0):
        sweep(b, 2, coef, FINE_HALO, -halo, L + halo, lambda z, cur, new: 2.0 * new - cur)
    for z in range(L):
        d[z] = c[z + 4] + b[z + 2]


def coarse_kernel(own, outer, inner, coef):
    def get(k, z):
        at = FIRST - (4 - k) * COARSE_HALO
        return ext(own, outer, inner, z, at, at, (3 + k) * L)

    for z in range(-COARSE_HALO, L + COARSE_HALO):
        vz = get(1, z)
        if not 0 <= z < L:
            vz = -vz
        write_coefs(coef, z + COARSE_HALO, get(0, z), vz, get(2, z), get(3, z), 2.0 * STEP)


def slab_pack_kernel(g, outer, inner):
    at = 0
    for k, count in enumerate((6, 4, 2)):
        for i in range(count):
            outer[at] = g[k, i]
            inner[at] = g[k, L - 1 - i]
            at += 1


def slab_kernel(g, outer, inner, coef, phi, total, relay, prefix, leaving, v):
    place = lax.axis_index("tm") % 4
    for z in range(-6, L + 6):
        v[z + 6] = ext(g.at[0], outer, inner, z)
    for z in range(L):
        leaving[z] = phi[z]

    def keep(wanted):
        @pl.when(place == wanted)
        def _():
            for z in range(-3, L + 3):
                prefix[z + 3] = v[z + 6]

    @pl.when(place < 2)
    def _():
        for z in range(L + 6):
            prefix[z] = jnp.zeros((NY, NX), jnp.float32)

    keep(2)
    coarse_twice(v, 6, coef, 6)
    for z in range(-4, L + 4):
        v[z + 6] += ext(g.at[1], outer, inner, z, 6, 6)
    keep(3)
    coarse_twice(v, 6, coef, 4)
    for z in range(-2, L + 2):
        v[z + 6] += ext(g.at[2], outer, inner, z, 10, 10)

    @pl.when(place == 0)
    def _():
        for z in range(L):
            relay[z] = v[z + 6]

    coarse_twice(v, 6, coef, 2)
    for z in range(L):
        total[z] = v[z + 6] + g[3, z]
        relay[L + z] = g[3, z]

    @pl.when(place > 0)
    def _():
        for z in range(L):
            relay[z] = total[z]


def chain1_kernel(far, pair, middle, shifted, own, coef, far_outer, outer, inner, psi, u):
    place = lax.axis_index("tm") % 4
    other = 1 - lax.axis_index("space") % 2
    for i in range(L):
        u[L - 1 - i] = far_outer[i]
        u[L + i] = far[i]
        u[2 * L + i] = pair[other, L - 1 - i]
        psi[i] = shifted[i] + own[L + i]
    for i in range(4):
        if i < 3:

            @pl.when(place >= 3 - i)
            def _():
                coarse_twice(u, L, coef, 8 - 2 * i)
        else:
            coarse_twice(u, L, coef, 2)

    @pl.when(place == 3)
    def _():
        for z in range(L):
            u[L + z] += middle[z]

    for z in range(L):
        outer[z] = u[L + z]
        inner[z] = u[L + L - 1 - z]
    for i in range(6):
        outer[L + i] = middle[i]
        inner[L + i] = middle[L - 1 - i]


def chain2_kernel(held, outer, inner, middle, relay, psi, coef, mine, to_outer, to_inner, u):
    place = lax.axis_index("tm") % 4
    for z in range(-L, 2 * L):
        u[L + z] = ext(held, outer, inner, z)
    for i in range(4):
        halo = 6 - 2 * i
        coarse_twice(u, L, coef, halo + 2)

        @pl.when(place == (2 - i) % 4)
        def _():
            for z in range(-halo, L + halo):
                u[L + z] += ext(relay, None, None, z) if i == 3 else ext(middle, outer, inner, z, L, L)

    for z in range(L):
        mine[z] = u[L + z]
        mine[L + z] = psi[z]
    for i in range(7):
        to_outer[i] = u[L + i]
        to_inner[i] = u[2 * L - 1 - i]
    for i in range(5):
        to_outer[7 + i] = relay[i]
        to_inner[7 + i] = relay[L - 1 - i]
    for i in range(3):
        to_outer[12 + i] = mine[L + i]
        to_inner[12 + i] = mine[2 * L - 1 - i]


def finish_kernel(mine, outer, inner, relay, prefix, g, phi, own, f_outer, f_inner, coef, fine, out, u, w):
    place = lax.axis_index("tm") % 4
    odd = lax.axis_index("space") % 2
    for z in range(-7, L + 7):
        u[7 + z] = ext(mine, outer, inner, z)

    def add_relay(halo):
        for z in range(-halo, L + halo):
            u[7 + z] += ext(relay, outer, inner, z, 7, 7)

    sweep(u, 7, coef, COARSE_HALO, -6, L + 6)
    sweep(u, 7, coef, COARSE_HALO, -5, L + 5)

    @pl.when(place == 2)
    def _():
        add_relay(5)

    sweep(u, 7, coef, COARSE_HALO, -4, L + 4)
    sweep(u, 7, coef, COARSE_HALO, -3, L + 3)

    @pl.when(place < 2)
    def _():
        add_relay(3)

    for z in range(-3, L + 3):
        g_t = u[7 + z] + prefix[3 + z]
        w[3 + z] = g_t
        u[7 + z] = g_t + ext(mine, outer, inner, z, 12, 12, L)
    coarse_twice(w, 3, coef, 2)

    @pl.when(place == 0)
    def _():
        for z in range(L):
            out[3, z + odd * (L - 1 - 2 * z)] = w[3 + z] + phi[z] + relay[L + z]

    @pl.when(place > 0)
    def _():
        for z in range(L):
            out[3, z + odd * (L - 1 - 2 * z)] = w[3 + z] + phi[z] + g[place - 1, z]

    at = SENT[0] + SENT[1]
    for step in range(3):
        halo = 2 - step
        sweep(u, 7, fine, FINE_HALO, -halo, L + halo,
              lambda z, cur, new: new + ext(own, f_outer, f_inner, z, at, at, 2 * L))
        for z in range(L):
            out[step, z + odd * (L - 1 - 2 * z)] = u[7 + z]


def body(guesses, forcing, initial, kappa, velocity):
    count, times = lax.axis_size("space"), lax.axis_size("tm")
    facing = [(i, i + 1) for i in range(1, count - 1, 2)]
    facing += [(b, a) for a, b in facing]
    paired = [(i, i ^ 1) for i in range(count)]

    def from_outer(x):
        return lax.ppermute(x, "space", facing)

    def from_inner(x):
        return lax.ppermute(x, "space", paired)

    def later(x, steps, moves=None):
        moves = [(i, i) for i in range(count)] if moves is None else moves
        pairs = [(t * count + a, (t + steps) * count + b) for t in range(times - steps) for a, b in moves]
        return lax.ppermute(x, ("tm", "space"), pairs)

    own, outer, inner = pl.pallas_call(
        pack_kernel,
        out_shape=[jax.ShapeDtypeStruct((n, NY, NX), jnp.float32) for n in (7 * L, FIRST, FIRST)],
        in_specs=[pl.BlockSpec(memory_space=pltpu.HBM)] * 5,
        scratch_shapes=[VMEM((7, L, NY, NX), jnp.float32), pltpu.SemaphoreType.DMA((7,))],
    )(guesses, forcing, initial, kappa, velocity)
    outer, inner = from_outer(outer), from_inner(inner)
    (own,) = call(settle_kernel, (7 * L,))(own)
    d, phi, fine = call(local_kernel, (L, L, (7, L + 2 * FINE_HALO)), (L + 8, L + 12, L + 4))(own, outer, inner)
    (coef,) = call(coarse_kernel, ((7, L + 2 * COARSE_HALO),))(own, outer, inner)
    groups = [[4 * a + b for b in range(4)] for a in range(times // 4)]
    g = lax.all_gather(d, "tm", axis_index_groups=groups)
    slab_outer, slab_inner = call(slab_pack_kernel, (12, 12))(g)
    slab_outer, slab_inner = from_outer(slab_outer), from_inner(slab_inner)
    total, relay, prefix, leaving = call(slab_kernel, (L, 2 * L, L + 6, L), (L + 12,))(
        g, slab_outer, slab_inner, coef, phi
    )
    shifted = later(leaving, 1)
    relay = later(relay, 4)
    middle = later(total, 8)
    far_outer = later(total, 12, facing)
    far = later(total, 12)
    pair = lax.all_gather(far, "space", axis_index_groups=[[i, i + 1] for i in range(0, count, 2)])
    c1_outer, c1_inner, psi = call(chain1_kernel, (L + 6, L + 6, L), (3 * L,))(
        far, pair, middle, shifted, own, coef, far_outer
    )
    mine, c2_outer, c2_inner = call(chain2_kernel, (2 * L, 15, 15), (3 * L,))(
        c1_outer, from_outer(c1_outer), from_inner(c1_inner), middle, relay, psi, coef
    )
    (out,) = call(finish_kernel, ((4, L),), (L + 14, L + 6))(
        mine, from_outer(c2_outer), from_inner(c2_inner), relay, prefix, g, phi, own, outer, inner, coef, fine
    )
    return out


def solution(mesh):
    placed = (
        P("tm", "space", None, None),
        P("tm", "space", None, None),
        P("space", None, None),
        P("space", None, None),
        P(None, "space", None, None),
    )
    return jax.shard_map(
        body, mesh=mesh, in_specs=placed, out_specs=P("tm", "space", None, None), check_vma=False
    )
```

```python
import functools

import jax
import jax.numpy as jnp
from jax import lax
from jax.experimental import pallas as pl
from jax.experimental.pallas import tpu as pltpu
from jax.sharding import PartitionSpec as P


L = 8
NY, NX = 32, 128
STEP = 0.3
FINE_HALO = 6
COARSE_HALO = 7
SENT = (4, 7, 6, COARSE_HALO)
FIRST = SENT[0] + SENT[1] + SENT[2] + 4 * COARSE_HALO
VMEM = pltpu.VMEM


def call(kernel, outs, scratch=()):
    return pl.pallas_call(
        kernel,
        out_shape=[jax.ShapeDtypeStruct((n, NY, NX) if isinstance(n, int) else n + (NY, NX), jnp.float32) for n in outs],
        scratch_shapes=[VMEM((n, NY, NX), jnp.float32) for n in scratch],
        compiler_params=pltpu.CompilerParams(vmem_limit_bytes=40 << 20),
    )


def stencil(u, at, cur, prev, nxt, coef, k):
    return (
        coef[0, k] * nxt
        + coef[1, k] * prev
        + coef[2, k] * pltpu.roll(cur, NY - 1, 0)
        + coef[3, k] * pltpu.roll(cur, 1, 0)
        + coef[4, k] * pltpu.roll(cur, NX - 1, 1)
        + coef[5, k] * pltpu.roll(cur, 1, 1)
        + coef[6, k] * cur
    )


def sweep(u, base, coef, coef_base, lo, hi, after=None):
    prev, cur = u[lo - 1 + base], u[lo + base]
    for z in range(lo, hi):
        nxt = u[z + 1 + base]
        new = stencil(u, z, cur, prev, nxt, coef, z + coef_base)
        u[z + base] = new if after is None else after(z, cur, new)
        prev, cur = cur, nxt


def coarse_twice(u, base, coef, halo):
    sweep(u, base, coef, COARSE_HALO, 1 - halo, L + halo - 1)
    sweep(u, base, coef, COARSE_HALO, 2 - halo, L + halo - 2)


def ext(own, outer, inner, z, outer_at=0, inner_at=0, own_at=0):
    if z < 0:
        return outer[outer_at - 1 - z]
    if z >= L:
        return inner[inner_at + z - L]
    return own[own_at + z]


def write_coefs(out, index, diffuse, vz, vy, vx, h):
    row = lax.broadcasted_iota(jnp.int32, (NY, NX), 0)
    lane = lax.broadcasted_iota(jnp.int32, (NY, NX), 1)
    zero = jnp.zeros((NY, NX), jnp.float32)

    def pair(v):
        return h * (diffuse - jnp.minimum(v, 0.0)), h * (diffuse + jnp.maximum(v, 0.0))

    (above_z, below_z), (above_y, below_y), (above_x, below_x) = pair(vz), pair(vy), pair(vx)
    out[0, index] = above_z
    out[1, index] = below_z
    out[2, index] = jnp.where(row == NY - 1, zero, above_y)
    out[3, index] = jnp.where(row == 0, zero, below_y)
    out[4, index] = jnp.where(lane == NX - 1, zero, above_x)
    out[5, index] = jnp.where(lane == 0, zero, below_x)
    out[6, index] = 1.0 - (above_z + below_z + above_y + below_y + above_x + below_x)


def pack_kernel(guesses, forcing, initial, kappa, velocity, own, outer, inner, held, sems):
    odd = lax.axis_index("space") % 2
    first = (lax.axis_index("tm") == 0).astype(jnp.float32)
    sign = (1 - 2 * odd).astype(jnp.float32)
    sources = (guesses.at[0], initial, forcing.at[0], kappa, velocity.at[0], velocity.at[1], velocity.at[2])
    copies = [pltpu.make_async_copy(source, held.at[k], sems.at[k]) for k, source in enumerate(sources)]
    for copy in copies:
        copy.start()
    at = 0
    for field, copy in enumerate(copies):
        copy.wait()
        for z in range(L):
            value = held[field, z + odd * (L - 1 - 2 * z)]
            if field in (1, 2, 4):
                value = (None, first, STEP, None, sign)[field] * value
            own[field * L + z] = value
        count = SENT[min(field, 3)]
        for i in range(count):
            outer[at + i] = own[field * L + i]
            inner[at + i] = own[field * L + L - 1 - i]
        at += count


def settle_kernel(held, own):
    for i in range(7 * L):
        own[i] = held[i]


def local_kernel(own, outer, inner, d, phi, coef, c, y, b):
    starts = (0, SENT[0], SENT[0] + SENT[1], SENT[0] + SENT[1] + SENT[2])

    def get(field, z):
        at = starts[min(field, 3)] + max(field - 3, 0) * COARSE_HALO
        return ext(own, outer, inner, z, at, at, field * L)

    for z in range(-FINE_HALO, L + FINE_HALO):
        vz = get(4, z)
        if not 0 <= z < L:
            vz = -vz
        write_coefs(coef, z + FINE_HALO, get(3, z), vz, get(5, z), get(6, z), STEP)
    for z in range(-7, L + 7):
        y[z + 7] = get(1, z)
    for z in range(-4, L + 4):
        c[z + 4] = get(0, z)
    for step in range(4):
        halo = 6 - step
        sweep(y, 7, coef, FINE_HALO, -halo, L + halo, lambda z, cur, new: new + get(2, z))
        halo = 3 - step
        sweep(c, 4, coef, FINE_HALO, -halo, L + halo)
    for z in range(-2, L + 2):
        b[z + 2] = y[z + 7] - get(0, z)
    for z in range(-3, L + 3):
        phi[z + 3] = y[z + 7]
    for halo in (1, 0):
        sweep(b, 2, coef, FINE_HALO, -halo, L + halo, lambda z, cur, new: 2.0 * new - cur)
    for z in range(L):
        d[z] = c[z + 4] + b[z + 2]
        phi[L + 6 + z] = d[z]


def coarse_kernel(own, outer, inner, coef):
    def get(k, z):
        at = FIRST - (4 - k) * COARSE_HALO
        return ext(own, outer, inner, z, at, at, (3 + k) * L)

    for z in range(-COARSE_HALO, L + COARSE_HALO):
        vz = get(1, z)
        if not 0 <= z < L:
            vz = -vz
        write_coefs(coef, z + COARSE_HALO, get(0, z), vz, get(2, z), get(3, z), 2.0 * STEP)


def slab_pack_kernel(g, outer, inner):
    at = 0
    for k, count in enumerate((6, 4, 2)):
        for i in range(count):
            outer[at] = g[k, i]
            inner[at] = g[k, L - 1 - i]
            at += 1


def slab_kernel(g, outer, inner, coef, total, partial, prefix, v):
    place = lax.axis_index("tm") % 4
    for z in range(-6, L + 6):
        v[z + 6] = ext(g.at[0], outer, inner, z)

    def keep(wanted):
        @pl.when(place == wanted)
        def _():
            for z in range(-3, L + 3):
                prefix[z + 3] = v[z + 6]

    @pl.when(place < 2)
    def _():
        for z in range(L + 6):
            prefix[z] = jnp.zeros((NY, NX), jnp.float32)

    keep(2)
    coarse_twice(v, 6, coef, 6)
    for z in range(-4, L + 4):
        v[z + 6] += ext(g.at[1], outer, inner, z, 6, 6)
    keep(3)
    coarse_twice(v, 6, coef, 4)
    for z in range(-2, L + 2):
        v[z + 6] += ext(g.at[2], outer, inner, z, 10, 10)
    for z in range(L):
        partial[z] = v[z + 6]
    coarse_twice(v, 6, coef, 2)
    for z in range(L):
        total[z] = v[z + 6] + g[3, z]


def arrived(block, outer, pair):
    other = 1 - lax.axis_index("space") % 2
    return lambda z: outer[-1 - z] if z < 0 else pair[other, 2 * L - 1 - z] if z >= L else block[z]


def chain1_kernel(block, outer, pair, total, partial, leaving, coef, to_next, opening, left, u):
    here = lax.axis_index("tm") // 4 == 1
    get = arrived(block, outer, pair)
    for i in range(2 * L + 6):
        left[i] = leaving[i]

    @pl.when(here)
    def _():
        for z in range(-L, 2 * L):
            u[L + z] = get(z)
        for i in range(3):
            coarse_twice(u, L, coef, 8 - 2 * i)
        for z in range(L):
            opening[z] = u[L + z] + partial[z]
        coarse_twice(u, L, coef, 2)
        for z in range(L):
            to_next[z] = u[L + z] + total[z]

    @pl.when(jnp.logical_not(here))
    def _():
        for z in range(L):
            opening[z] = partial[z]
            to_next[z] = total[z]


def chain2_kernel(block, outer, pair, total, partial, opening, coef, to_next, u):
    here = lax.axis_index("tm") // 4 == 2
    leads = lax.axis_index("tm") % 4 == 0
    get = arrived(block, outer, pair)

    @pl.when(here)
    def _():
        for z in range(-L, 2 * L):
            u[L + z] = get(z)
        for i in range(3):
            coarse_twice(u, L, coef, 8 - 2 * i)

        @pl.when(leads)
        def _():
            for z in range(L):
                to_next[z] = u[L + z] + partial[z]

        @pl.when(jnp.logical_not(leads))
        def _():
            coarse_twice(u, L, coef, 2)
            for z in range(L):
                to_next[z] = u[L + z] + total[z]

    @pl.when(jnp.logical_not(here))
    def _():
        for z in range(L):
            to_next[z] = opening[z]


def finish_kernel(b1, o1, p1, b2, o2, p2, b3, o3, p3, before, prefix, phi, own, outer, inner, coef, fine, out, u, w):
    group, place = lax.axis_index("tm") // 4, lax.axis_index("tm") % 4
    first = lax.axis_index("tm") == 0
    odd = lax.axis_index("space") % 2

    def load(wanted, get):
        @pl.when(wanted)
        def _():
            for z in range(-7, L + 7):
                u[7 + z] = get(z)

    last = jnp.logical_or(place == 0, jnp.logical_or(group == 0, group == 3))
    load(last, arrived(b3, o3, p3))
    load(jnp.logical_and(jnp.logical_not(last), group == 1), arrived(b1, o1, p1))
    load(jnp.logical_and(jnp.logical_not(last), group == 2), arrived(b2, o2, p2))

    @pl.when(place == 3)
    def _():
        sweep(u, 7, coef, COARSE_HALO, -6, L + 6)
        sweep(u, 7, coef, COARSE_HALO, -5, L + 5)

    @pl.when(place >= 2)
    def _():
        sweep(u, 7, coef, COARSE_HALO, -4, L + 4)
        sweep(u, 7, coef, COARSE_HALO, -3, L + 3)

    for z in range(-3, L + 3):
        w[3 + z] = u[7 + z] + prefix[3 + z]

    @pl.when(first)
    def _():
        for z in range(-3, L + 3):
            u[7 + z] = w[3 + z] + ext(own, outer, inner, z, SENT[0], SENT[0], L)

    @pl.when(jnp.logical_not(first))
    def _():
        for z in range(-3, L + 3):
            u[7 + z] = w[3 + z] + before[3 + z]

    coarse_twice(w, 3, coef, 2)
    for z in range(L):
        out[3, z + odd * (L - 1 - 2 * z)] = w[3 + z] + before[L + 6 + z] + phi[3 + z]
    at = SENT[0] + SENT[1]
    for step in range(3):
        halo = 2 - step
        sweep(u, 7, fine, FINE_HALO, -halo, L + halo,
              lambda z, cur, new: new + ext(own, outer, inner, z, at, at, 2 * L))
        for z in range(L):
            out[step, z + odd * (L - 1 - 2 * z)] = u[7 + z]


def body(guesses, forcing, initial, kappa, velocity):
    count, times = lax.axis_size("space"), lax.axis_size("tm")
    facing = [(i, i + 1) for i in range(1, count - 1, 2)]
    facing += [(b, a) for a, b in facing]
    paired = [(i, i ^ 1) for i in range(count)]

    def from_outer(x):
        return lax.ppermute(x, "space", facing)

    def from_inner(x):
        return lax.ppermute(x, "space", paired)

    def later(x, steps, moves=None, leaving=range(times)):
        moves = [(i, i) for i in range(count)] if moves is None else moves
        pairs = [(t * count + a, (t + steps) * count + b) for t in leaving if t + steps < times for a, b in moves]
        return lax.ppermute(x, ("tm", "space"), pairs)

    def hand_on(x, leaving):
        block, outer = later(x, 4, None, leaving), later(x, 4, facing, leaving)
        pair = lax.all_gather(block, "space", axis_index_groups=[[i, i + 1] for i in range(0, count, 2)])
        return block, outer, pair

    own, outer, inner = pl.pallas_call(
        pack_kernel,
        out_shape=[jax.ShapeDtypeStruct((n, NY, NX), jnp.float32) for n in (7 * L, FIRST, FIRST)],
        in_specs=[pl.BlockSpec(memory_space=pltpu.HBM)] * 5,
        scratch_shapes=[VMEM((7, L, NY, NX), jnp.float32), pltpu.SemaphoreType.DMA((7,))],
    )(guesses, forcing, initial, kappa, velocity)
    outer, inner = from_outer(outer), from_inner(inner)
    (own,) = call(settle_kernel, (7 * L,))(own)
    d, phi, fine = call(local_kernel, (L, 2 * L + 6, (7, L + 2 * FINE_HALO)), (L + 8, L + 14, L + 4))(own, outer, inner)
    (coef,) = call(coarse_kernel, ((7, L + 2 * COARSE_HALO),))(own, outer, inner)
    g = lax.all_gather(d, "tm", axis_index_groups=[[4 * a + b for b in range(4)] for a in range(times // 4)])
    slab_outer, slab_inner = call(slab_pack_kernel, (12, 12))(g)
    slab_outer, slab_inner = from_outer(slab_outer), from_inner(slab_inner)
    total, partial, prefix = call(slab_kernel, (L, L, L + 6), (L + 12,))(g, slab_outer, slab_inner, coef)
    one = hand_on(total, range(4))
    to_two, opening, left = call(chain1_kernel, (L, L, 2 * L + 6), (3 * L,))(*one, total, partial, phi, coef)
    before = later(left, 1)
    two = hand_on(to_two, range(4, 8))
    (to_three,) = call(chain2_kernel, (L,), (3 * L,))(*two, total, partial, opening, coef)
    three = hand_on(to_three, (0, 4, 8, 9, 10, 11))
    (out,) = call(finish_kernel, ((4, L),), (L + 14, L + 6))(
        *one, *two, *three, before, prefix, phi, own, outer, inner, coef, fine
    )
    return out


def solution(mesh):
    placed = (
        P("tm", "space", None, None),
        P("tm", "space", None, None),
        P("space", None, None),
        P("space", None, None),
        P(None, "space", None, None),
    )
    return jax.shard_map(
        body, mesh=mesh, in_specs=placed, out_specs=P("tm", "space", None, None), check_vma=False
    )
```

```python
import functools

import jax
import jax.numpy as jnp
from jax import lax
from jax.experimental import pallas as pl
from jax.experimental.pallas import tpu as pltpu
from jax.sharding import PartitionSpec as P


L = 8
NY, NX = 32, 128
STEP = 0.3
FINE_HALO = 6
COARSE_HALO = 7
SENT = (4, 6, COARSE_HALO)
COEFS = SENT[0] + SENT[1]
FIRST = COEFS + 4 * COARSE_HALO
OPEN = 7
VMEM = pltpu.VMEM


def call(kernel, outs, scratch=()):
    return pl.pallas_call(
        kernel,
        out_shape=[jax.ShapeDtypeStruct((n, NY, NX) if isinstance(n, int) else n + (NY, NX), jnp.float32) for n in outs],
        scratch_shapes=[VMEM((n, NY, NX), jnp.float32) for n in scratch],
        compiler_params=pltpu.CompilerParams(vmem_limit_bytes=40 << 20),
    )


def stencil(u, at, cur, prev, nxt, coef, k):
    return (
        coef[0, k] * nxt
        + coef[1, k] * prev
        + coef[2, k] * pltpu.roll(cur, NY - 1, 0)
        + coef[3, k] * pltpu.roll(cur, 1, 0)
        + coef[4, k] * pltpu.roll(cur, NX - 1, 1)
        + coef[5, k] * pltpu.roll(cur, 1, 1)
        + coef[6, k] * cur
    )


def sweep(u, base, coef, coef_base, lo, hi, after=None):
    prev, cur = u[lo - 1 + base], u[lo + base]
    for z in range(lo, hi):
        nxt = u[z + 1 + base]
        new = stencil(u, z, cur, prev, nxt, coef, z + coef_base)
        u[z + base] = new if after is None else after(z, cur, new)
        prev, cur = cur, nxt


def coarse_twice(u, base, coef, halo):
    sweep(u, base, coef, COARSE_HALO, 1 - halo, L + halo - 1)
    sweep(u, base, coef, COARSE_HALO, 2 - halo, L + halo - 2)


def ext(own, outer, inner, z, outer_at=0, inner_at=0, own_at=0):
    if z < 0:
        return outer[outer_at - 1 - z]
    if z >= L:
        return inner[inner_at + z - L]
    return own[own_at + z]


def write_coefs(out, index, diffuse, vz, vy, vx, h):
    row = lax.broadcasted_iota(jnp.int32, (NY, NX), 0)
    lane = lax.broadcasted_iota(jnp.int32, (NY, NX), 1)
    zero = jnp.zeros((NY, NX), jnp.float32)

    def pair(v):
        return h * (diffuse - jnp.minimum(v, 0.0)), h * (diffuse + jnp.maximum(v, 0.0))

    (above_z, below_z), (above_y, below_y), (above_x, below_x) = pair(vz), pair(vy), pair(vx)
    out[0, index] = above_z
    out[1, index] = below_z
    out[2, index] = jnp.where(row == NY - 1, zero, above_y)
    out[3, index] = jnp.where(row == 0, zero, below_y)
    out[4, index] = jnp.where(lane == NX - 1, zero, above_x)
    out[5, index] = jnp.where(lane == 0, zero, below_x)
    out[6, index] = 1.0 - (above_z + below_z + above_y + below_y + above_x + below_x)


def pack_kernel(
    guesses, forcing, kappa, velocity, initial, own, outer, inner, open_outer, open_inner, held, kept, low, high, sems, out_sems
):
    odd = lax.axis_index("space") % 2
    first = (lax.axis_index("tm") == 0).astype(jnp.float32)
    scale = (None, STEP, None, (1 - 2 * odd).astype(jnp.float32), None, None, first)
    sources = (guesses.at[0], forcing.at[0], kappa, velocity.at[0], velocity.at[1], velocity.at[2], initial)
    copies = [pltpu.make_async_copy(source, held.at[k], sems.at[k]) for k, source in enumerate(sources)]
    for copy in copies:
        copy.start()
    leaving, at = [], 0
    for field, copy in enumerate(copies):
        copy.wait()
        for z in range(L):
            value = held[field, z + odd * (L - 1 - 2 * z)]
            kept[field * L + z] = value if scale[field] is None else scale[field] * value
        count = SENT[min(field, 2)] if field < 6 else OPEN
        for i in range(count):
            low[at + i] = kept[field * L + i]
            high[at + i] = kept[field * L + L - 1 - i]
        spots, block = pl.ds(at, count), pl.ds(field * L, L)
        for k, (source, to) in enumerate((
            (low.at[spots], outer.at[spots] if field < 6 else open_outer),
            (high.at[spots], inner.at[spots] if field < 6 else open_inner),
            (kept.at[block], own.at[block]),
        )):
            leaving.append(pltpu.make_async_copy(source, to, out_sems.at[3 * field + k]))
            leaving[-1].start()
        at += count
    for copy in leaving:
        copy.wait()


def settle_kernel(held, own):
    for i in range(7 * L):
        own[i] = held[i]


def local_kernel(own, outer, inner, open_outer, open_inner, d, phi, coef, c, y, b):
    def get(field, z):
        if field == 6:
            return ext(own, open_outer, open_inner, z, 0, 0, 6 * L)
        at = (0, SENT[0], *range(COEFS, FIRST, COARSE_HALO))[field]
        return ext(own, outer, inner, z, at, at, field * L)

    for z in range(-FINE_HALO, L + FINE_HALO):
        vz = get(3, z)
        if not 0 <= z < L:
            vz = -vz
        write_coefs(coef, z + FINE_HALO, get(2, z), vz, get(4, z), get(5, z), STEP)
    for z in range(-7, L + 7):
        y[z + 7] = get(6, z)
    for z in range(-4, L + 4):
        c[z + 4] = get(0, z)
    for step in range(4):
        halo = 6 - step
        sweep(y, 7, coef, FINE_HALO, -halo, L + halo, lambda z, cur, new: new + get(1, z))
        halo = 3 - step
        sweep(c, 4, coef, FINE_HALO, -halo, L + halo)
    for z in range(-2, L + 2):
        b[z + 2] = y[z + 7] - get(0, z)
    for z in range(-3, L + 3):
        phi[z + 3] = y[z + 7]
    for halo in (1, 0):
        sweep(b, 2, coef, FINE_HALO, -halo, L + halo, lambda z, cur, new: 2.0 * new - cur)
    for z in range(L):
        d[z] = c[z + 4] + b[z + 2]


def coarse_kernel(own, outer, inner, coef):
    def get(k, z):
        at = COEFS + k * COARSE_HALO
        return ext(own, outer, inner, z, at, at, (2 + k) * L)

    for z in range(-COARSE_HALO, L + COARSE_HALO):
        vz = get(1, z)
        if not 0 <= z < L:
            vz = -vz
        write_coefs(coef, z + COARSE_HALO, get(0, z), vz, get(2, z), get(3, z), 2.0 * STEP)


def slab_pack_kernel(g, outer, inner):
    at = 0
    for k, count in enumerate((6, 4, 2)):
        for i in range(count):
            outer[at] = g[k, i]
            inner[at] = g[k, L - 1 - i]
            at += 1


def slab_kernel(g, outer, inner, coef, total, partial, prefix, v):
    place = lax.axis_index("tm") % 4
    for z in range(-6, L + 6):
        v[z + 6] = ext(g.at[0], outer, inner, z)

    def keep(wanted):
        @pl.when(place == wanted)
        def _():
            for z in range(-3, L + 3):
                prefix[z + 3] = v[z + 6]

    @pl.when(place < 2)
    def _():
        for z in range(L + 6):
            prefix[z] = jnp.zeros((NY, NX), jnp.float32)

    keep(2)
    coarse_twice(v, 6, coef, 6)
    for z in range(-4, L + 4):
        v[z + 6] += ext(g.at[1], outer, inner, z, 6, 6)
    keep(3)
    coarse_twice(v, 6, coef, 4)
    for z in range(-2, L + 2):
        v[z + 6] += ext(g.at[2], outer, inner, z, 10, 10)
    for z in range(L):
        partial[z] = v[z + 6]
    coarse_twice(v, 6, coef, 2)
    for z in range(L):
        total[z] = v[z + 6] + g[3, z]


def arrived(block, outer, pair):
    other = 1 - lax.axis_index("space") % 2
    return lambda z: outer[-1 - z] if z < 0 else pair[other, 2 * L - 1 - z] if z >= L else block[z]


def leave_kernel(phi, total, leaving):
    for i in range(L + 6):
        leaving[i] = phi[i]


def chain1_kernel(block, outer, pair, total, partial, d, coef, opening, send, u):
    here = lax.axis_index("tm") // 4 == 1
    get = arrived(block, outer, pair)

    @pl.when(here)
    def _():
        for z in range(-L, 2 * L):
            u[L + z] = get(z)
        for i in range(3):
            coarse_twice(u, L, coef, 8 - 2 * i)
        for z in range(L):
            opening[z] = u[L + z] + partial[z]
        coarse_twice(u, L, coef, 2)
        for z in range(L):
            send[z] = u[L + z] + total[z]

    @pl.when(jnp.logical_not(here))
    def _():
        for z in range(L):
            opening[z] = partial[z]
            send[z] = d[z]

    @pl.when(lax.axis_index("tm") // 4 == 0)
    def _():
        for z in range(L):
            send[z] = partial[z]


def chain2_kernel(block, outer, pair, total, partial, opening, coef, send, u):
    here, place = lax.axis_index("tm") // 4 == 2, lax.axis_index("tm") % 4
    get = arrived(block, outer, pair)

    @pl.when(here)
    def _():
        for z in range(-L, 2 * L):
            u[L + z] = get(z)
        for i in range(3):
            coarse_twice(u, L, coef, 8 - 2 * i)

        @pl.when(place == 0)
        def _():
            for z in range(L):
                send[z] = u[L + z] + partial[z]

        @pl.when(place > 0)
        def _():
            coarse_twice(u, L, coef, 2)
            for z in range(L):
                send[z] = u[L + z] + total[z]

    @pl.when(jnp.logical_not(here))
    def _():
        for z in range(L):
            send[z] = opening[z]


def finish_kernel(b1, o1, p1, b2, o2, p2, b3, o3, p3, before, g, prefix, phi, own, outer, inner, open_outer, open_inner, coef, fine, out, u, w):
    t = lax.axis_index("tm")
    group, place = t // 4, t % 4
    odd = lax.axis_index("space") % 2

    def put(wanted, into, halo, get):
        @pl.when(wanted)
        def _():
            for z in range(-halo, L + halo):
                into[halo + z] = get(z)

    source = jnp.where(jnp.logical_and(place == 0, group > 0), jnp.minimum(group + 1, 3), group)
    put(source == 0, u, 7, lambda z: jnp.zeros((NY, NX), jnp.float32))
    put(source == 1, u, 7, arrived(b1, o1, p1))
    put(source == 2, u, 7, arrived(b2, o2, p2))
    put(source == 3, u, 7, arrived(b3, o3, p3))
    @pl.when(place == 3)
    def _():
        sweep(u, 7, coef, COARSE_HALO, -6, L + 6)
        sweep(u, 7, coef, COARSE_HALO, -5, L + 5)

    @pl.when(place >= 2)
    def _():
        sweep(u, 7, coef, COARSE_HALO, -4, L + 4)
        sweep(u, 7, coef, COARSE_HALO, -3, L + 3)

    for z in range(-3, L + 3):
        w[3 + z] = u[7 + z] + prefix[3 + z]

    @pl.when(t == 0)
    def _():
        for z in range(-3, L + 3):
            u[7 + z] = w[3 + z] + ext(own, open_outer, open_inner, z, 0, 0, 6 * L)

    @pl.when(t > 0)
    def _():
        for z in range(-3, L + 3):
            u[7 + z] = w[3 + z] + before[3 + z]

    coarse_twice(w, 3, coef, 2)

    def last(wanted, get):
        @pl.when(wanted)
        def _():
            for z in range(L):
                out[3, z + odd * (L - 1 - 2 * z)] = get(z) + phi[3 + z]

    last(place > 0, lambda z: w[3 + z] + g[place - 1, z])
    last(t == 0, lambda z: w[3 + z])
    last(t == 4, lambda z: b1[z])
    last(t == 8, lambda z: b2[z])
    last(t == 12, lambda z: w[3 + z] + b2[z])
    at = SENT[0]
    for step in range(3):
        halo = 2 - step
        sweep(u, 7, fine, FINE_HALO, -halo, L + halo,
              lambda z, cur, new: new + ext(own, outer, inner, z, at, at, L))
        for z in range(L):
            out[step, z + odd * (L - 1 - 2 * z)] = u[7 + z]


def body(guesses, forcing, initial, kappa, velocity):
    count, times = lax.axis_size("space"), lax.axis_size("tm")
    facing = [(i, i + 1) for i in range(1, count - 1, 2)]
    facing += [(b, a) for a, b in facing]
    paired = [(i, i ^ 1) for i in range(count)]

    def from_outer(x):
        return lax.ppermute(x, "space", facing)

    def from_inner(x):
        return lax.ppermute(x, "space", paired)

    same = [(i, i) for i in range(count)]

    def move(x, intervals, moves=same):
        pairs = [(a * count + i, b * count + j) for a, b in intervals for i, j in moves]
        return lax.ppermute(x, ("tm", "space"), pairs)

    def hop(x, intervals, others=()):
        block, outer = move(x, [*intervals, *others]), move(x, intervals, facing)
        pair = lax.all_gather(block, "space", axis_index_groups=[[i, i + 1] for i in range(0, count, 2)])
        return block, outer, pair

    hbm = pl.BlockSpec(memory_space=pltpu.HBM)
    own, outer, inner, open_outer, open_inner = pl.pallas_call(
        pack_kernel,
        out_shape=[jax.ShapeDtypeStruct((n, NY, NX), jnp.float32) for n in (7 * L, FIRST, FIRST, OPEN, OPEN)],
        in_specs=[hbm] * 5,
        out_specs=[hbm] * 5,
        scratch_shapes=[
            VMEM((7, L, NY, NX), jnp.float32),
            *[VMEM((n, NY, NX), jnp.float32) for n in (7 * L, FIRST + OPEN, FIRST + OPEN)],
            pltpu.SemaphoreType.DMA((7,)),
            pltpu.SemaphoreType.DMA((21,)),
        ],
    )(guesses, forcing, kappa, velocity, initial)
    outer, inner = from_outer(outer), from_inner(inner)
    open_outer, open_inner = move(open_outer, [(0, 0)], facing), move(open_inner, [(0, 0)], paired)
    (own,) = call(settle_kernel, (7 * L,))(own)
    d, phi, fine = call(local_kernel, (L, L + 6, (7, L + 2 * FINE_HALO)), (L + 8, L + 14, L + 4))(
        own, outer, inner, open_outer, open_inner
    )
    (coef,) = call(coarse_kernel, ((7, L + 2 * COARSE_HALO),))(own, outer, inner)
    g = lax.all_gather(d, "tm", axis_index_groups=[[4 * a + b for b in range(4)] for a in range(times // 4)])
    slab_outer, slab_inner = call(slab_pack_kernel, (12, 12))(g)
    slab_outer, slab_inner = from_outer(slab_outer), from_inner(slab_inner)
    total, partial, prefix = call(slab_kernel, (L, L, L + 6), (L + 12,))(g, slab_outer, slab_inner, coef)

    def after(slab):
        return [(t, t + 4) for t in range(4 * slab, 4 * slab + 4)]

    one = hop(total, after(0))
    opening, send = call(chain1_kernel, (L, L), (3 * L,))(*one, total, partial, d, coef)
    (leaving,) = call(leave_kernel, (L + 6,))(phi, send)
    before = move(leaving, [(t, t + 1) for t in range(times - 1)])
    two = hop(send, after(1) + [(0, 4)], [(11, 12)])
    (send,) = call(chain2_kernel, (L,), (3 * L,))(*two, total, partial, opening, coef)
    three = hop(send, after(2) + [(4, 8)])
    (out,) = call(finish_kernel, ((4, L),), (L + 14, L + 6))(
        *one, *two, *three, before, g, prefix, phi, own, outer, inner, open_outer, open_inner, coef, fine
    )
    return out


def solution(mesh):
    placed = (
        P("tm", "space", None, None),
        P("tm", "space", None, None),
        P("space", None, None),
        P("space", None, None),
        P(None, "space", None, None),
    )
    return jax.shard_map(
        body, mesh=mesh, in_specs=placed, out_specs=P("tm", "space", None, None), check_vma=False
    )
```

```python
import functools

import jax
import jax.numpy as jnp
from jax import lax
from jax.experimental import pallas as pl
from jax.experimental.pallas import tpu as pltpu
from jax.sharding import PartitionSpec as P


L = 8
NY, NX = 32, 128
STEP = 0.3
FINE_HALO = 6
COARSE_HALO = 7
SENT = (4, 6, COARSE_HALO)
COEFS = SENT[0] + SENT[1]
FIRST = COEFS + 4 * COARSE_HALO
OPEN = 7
VMEM = pltpu.VMEM


def call(kernel, outs, scratch=()):
    return pl.pallas_call(
        kernel,
        out_shape=[jax.ShapeDtypeStruct((n, NY, NX) if isinstance(n, int) else n + (NY, NX), jnp.float32) for n in outs],
        scratch_shapes=[VMEM((n, NY, NX), jnp.float32) for n in scratch],
        compiler_params=pltpu.CompilerParams(vmem_limit_bytes=40 << 20),
    )


def stencil(u, at, cur, prev, nxt, coef, k):
    return (
        coef[0, k] * nxt
        + coef[1, k] * prev
        + coef[2, k] * pltpu.roll(cur, NY - 1, 0)
        + coef[3, k] * pltpu.roll(cur, 1, 0)
        + coef[4, k] * pltpu.roll(cur, NX - 1, 1)
        + coef[5, k] * pltpu.roll(cur, 1, 1)
        + coef[6, k] * cur
    )


def sweep(u, base, coef, coef_base, lo, hi, after=None):
    prev, cur = u[lo - 1 + base], u[lo + base]
    for z in range(lo, hi):
        nxt = u[z + 1 + base]
        new = stencil(u, z, cur, prev, nxt, coef, z + coef_base)
        u[z + base] = new if after is None else after(z, cur, new)
        prev, cur = cur, nxt


def coarse_twice(u, base, coef, halo):
    sweep(u, base, coef, COARSE_HALO, 1 - halo, L + halo - 1)
    sweep(u, base, coef, COARSE_HALO, 2 - halo, L + halo - 2)


def ext(own, outer, inner, z, outer_at=0, inner_at=0, own_at=0):
    if z < 0:
        return outer[outer_at - 1 - z]
    if z >= L:
        return inner[inner_at + z - L]
    return own[own_at + z]


def write_coefs(out, index, diffuse, vz, vy, vx, h):
    row = lax.broadcasted_iota(jnp.int32, (NY, NX), 0)
    lane = lax.broadcasted_iota(jnp.int32, (NY, NX), 1)
    zero = jnp.zeros((NY, NX), jnp.float32)

    def pair(v):
        return h * (diffuse - jnp.minimum(v, 0.0)), h * (diffuse + jnp.maximum(v, 0.0))

    (above_z, below_z), (above_y, below_y), (above_x, below_x) = pair(vz), pair(vy), pair(vx)
    out[0, index] = above_z
    out[1, index] = below_z
    out[2, index] = jnp.where(row == NY - 1, zero, above_y)
    out[3, index] = jnp.where(row == 0, zero, below_y)
    out[4, index] = jnp.where(lane == NX - 1, zero, above_x)
    out[5, index] = jnp.where(lane == 0, zero, below_x)
    out[6, index] = 1.0 - (above_z + below_z + above_y + below_y + above_x + below_x)


def pack_kernel(
    guesses, forcing, kappa, velocity, initial, own, outer, inner, open_outer, open_inner, held, kept, low, high, sems, out_sems
):
    odd = lax.axis_index("space") % 2
    first = (lax.axis_index("tm") == 0).astype(jnp.float32)
    scale = (None, STEP, None, (1 - 2 * odd).astype(jnp.float32), None, None, first)
    sources = (guesses.at[0], forcing.at[0], kappa, velocity.at[0], velocity.at[1], velocity.at[2], initial)
    copies = [pltpu.make_async_copy(source, held.at[k], sems.at[k]) for k, source in enumerate(sources)]
    for copy in copies:
        copy.start()
    leaving, at = [], 0
    for field, copy in enumerate(copies):
        copy.wait()
        for z in range(L):
            value = held[field, z + odd * (L - 1 - 2 * z)]
            kept[field * L + z] = value if scale[field] is None else scale[field] * value
        count = SENT[min(field, 2)] if field < 6 else OPEN
        for i in range(count):
            low[at + i] = kept[field * L + i]
            high[at + i] = kept[field * L + L - 1 - i]
        spots, block = pl.ds(at, count), pl.ds(field * L, L)
        for k, (source, to) in enumerate((
            (low.at[spots], outer.at[spots] if field < 6 else open_outer),
            (high.at[spots], inner.at[spots] if field < 6 else open_inner),
            (kept.at[block], own.at[block]),
        )):
            leaving.append(pltpu.make_async_copy(source, to, out_sems.at[3 * field + k]))
            leaving[-1].start()
        at += count
    for copy in leaving:
        copy.wait()


def settle_kernel(held, own):
    for i in range(7 * L):
        own[i] = held[i]


def local_kernel(own, outer, inner, open_outer, open_inner, d, phi, coef, c, y, b):
    def get(field, z):
        if field == 6:
            return ext(own, open_outer, open_inner, z, 0, 0, 6 * L)
        at = (0, SENT[0], *range(COEFS, FIRST, COARSE_HALO))[field]
        return ext(own, outer, inner, z, at, at, field * L)

    for z in range(-FINE_HALO, L + FINE_HALO):
        vz = get(3, z)
        if not 0 <= z < L:
            vz = -vz
        write_coefs(coef, z + FINE_HALO, get(2, z), vz, get(4, z), get(5, z), STEP)
    for z in range(-7, L + 7):
        y[z + 7] = get(6, z)
    for z in range(-4, L + 4):
        c[z + 4] = get(0, z)
    for step in range(4):
        halo = 6 - step
        sweep(y, 7, coef, FINE_HALO, -halo, L + halo, lambda z, cur, new: new + get(1, z))
        halo = 3 - step
        sweep(c, 4, coef, FINE_HALO, -halo, L + halo)
    for z in range(-2, L + 2):
        b[z + 2] = y[z + 7] - get(0, z)
    for z in range(-3, L + 3):
        phi[z + 3] = y[z + 7]
    for halo in (1, 0):
        sweep(b, 2, coef, FINE_HALO, -halo, L + halo, lambda z, cur, new: 2.0 * new - cur)
    for z in range(L):
        d[z] = c[z + 4] + b[z + 2]


def coarse_kernel(own, outer, inner, coef):
    def get(k, z):
        at = COEFS + k * COARSE_HALO
        return ext(own, outer, inner, z, at, at, (2 + k) * L)

    for z in range(-COARSE_HALO, L + COARSE_HALO):
        vz = get(1, z)
        if not 0 <= z < L:
            vz = -vz
        write_coefs(coef, z + COARSE_HALO, get(0, z), vz, get(2, z), get(3, z), 2.0 * STEP)


def slab_pack_kernel(g, outer, inner):
    at = 0
    for k, count in enumerate((6, 4, 2)):
        for i in range(count):
            outer[at] = g[k, i]
            inner[at] = g[k, L - 1 - i]
            at += 1


def slab_kernel(g, outer, inner, coef, total, partial, prefix, v):
    place = lax.axis_index("tm") % 4
    for z in range(-6, L + 6):
        v[z + 6] = ext(g.at[0], outer, inner, z)

    def keep(wanted):
        @pl.when(place == wanted)
        def _():
            for z in range(-3, L + 3):
                prefix[z + 3] = v[z + 6]

    @pl.when(place < 2)
    def _():
        for z in range(L + 6):
            prefix[z] = jnp.zeros((NY, NX), jnp.float32)

    keep(2)
    coarse_twice(v, 6, coef, 6)
    for z in range(-4, L + 4):
        v[z + 6] += ext(g.at[1], outer, inner, z, 6, 6)
    keep(3)
    coarse_twice(v, 6, coef, 4)
    for z in range(-2, L + 2):
        v[z + 6] += ext(g.at[2], outer, inner, z, 10, 10)
    for z in range(L):
        partial[z] = v[z + 6]
    coarse_twice(v, 6, coef, 2)
    for z in range(L):
        total[z] = v[z + 6] + g[3, z]


def arrived(block, outer, pair):
    other = 1 - lax.axis_index("space") % 2
    return lambda z: outer[-1 - z] if z < 0 else pair[other, 2 * L - 1 - z] if z >= L else block[z]


def leave_kernel(phi, total, leaving):
    for i in range(L + 6):
        leaving[i] = phi[i]


def chain1_kernel(block, outer, pair, total, partial, d, coef, opening, send, u):
    here = lax.axis_index("tm") // 4 == 1
    get = arrived(block, outer, pair)

    @pl.when(here)
    def _():
        for z in range(-L, 2 * L):
            u[L + z] = get(z)
        for i in range(3):
            coarse_twice(u, L, coef, 8 - 2 * i)
        for z in range(L):
            opening[z] = u[L + z] + partial[z]
        coarse_twice(u, L, coef, 2)
        for z in range(L):
            send[z] = u[L + z] + total[z]

    @pl.when(jnp.logical_not(here))
    def _():
        for z in range(L):
            opening[z] = partial[z]
            send[z] = d[z]

    @pl.when(lax.axis_index("tm") // 4 == 0)
    def _():
        for z in range(L):
            send[z] = partial[z]


def chain2_kernel(block, outer, pair, total, partial, opening, coef, before, send, kept, u):
    for i in range(L + 6):
        kept[i] = before[i]
    here, place = lax.axis_index("tm") // 4 == 2, lax.axis_index("tm") % 4
    get = arrived(block, outer, pair)

    @pl.when(here)
    def _():
        for z in range(-L, 2 * L):
            u[L + z] = get(z)
        for i in range(3):
            coarse_twice(u, L, coef, 8 - 2 * i)

        @pl.when(place == 0)
        def _():
            for z in range(L):
                send[z] = u[L + z] + partial[z]

        @pl.when(place > 0)
        def _():
            coarse_twice(u, L, coef, 2)
            for z in range(L):
                send[z] = u[L + z] + total[z]

    @pl.when(jnp.logical_not(here))
    def _():
        for z in range(L):
            send[z] = opening[z]


def finish_kernel(b1, o1, p1, b2, o2, p2, b3, o3, p3, before, g, prefix, phi, own, outer, inner, open_outer, open_inner, coef, fine, out, u, w):
    t = lax.axis_index("tm")
    group, place = t // 4, t % 4
    odd = lax.axis_index("space") % 2

    def put(wanted, into, halo, get):
        @pl.when(wanted)
        def _():
            for z in range(-halo, L + halo):
                into[halo + z] = get(z)

    source = jnp.where(jnp.logical_and(place == 0, group > 0), jnp.minimum(group + 1, 3), group)
    put(source == 0, u, 7, lambda z: jnp.zeros((NY, NX), jnp.float32))
    put(source == 1, u, 7, arrived(b1, o1, p1))
    put(source == 2, u, 7, arrived(b2, o2, p2))
    put(source == 3, u, 7, arrived(b3, o3, p3))
    @pl.when(place == 3)
    def _():
        sweep(u, 7, coef, COARSE_HALO, -6, L + 6)
        sweep(u, 7, coef, COARSE_HALO, -5, L + 5)

    @pl.when(place >= 2)
    def _():
        sweep(u, 7, coef, COARSE_HALO, -4, L + 4)
        sweep(u, 7, coef, COARSE_HALO, -3, L + 3)

    for z in range(-3, L + 3):
        w[3 + z] = u[7 + z] + prefix[3 + z]

    @pl.when(t == 0)
    def _():
        for z in range(-3, L + 3):
            u[7 + z] = w[3 + z] + ext(own, open_outer, open_inner, z, 0, 0, 6 * L)

    @pl.when(t > 0)
    def _():
        for z in range(-3, L + 3):
            u[7 + z] = w[3 + z] + before[3 + z]

    coarse_twice(w, 3, coef, 2)

    def last(wanted, get):
        @pl.when(wanted)
        def _():
            for z in range(L):
                out[3, z + odd * (L - 1 - 2 * z)] = get(z) + phi[3 + z]

    last(place > 0, lambda z: w[3 + z] + g[place - 1, z])
    last(t == 0, lambda z: w[3 + z])
    last(t == 4, lambda z: b1[z])
    last(t == 8, lambda z: b2[z])
    last(t == 12, lambda z: w[3 + z] + b2[z])
    at = SENT[0]
    for step in range(3):
        halo = 2 - step
        sweep(u, 7, fine, FINE_HALO, -halo, L + halo,
              lambda z, cur, new: new + ext(own, outer, inner, z, at, at, L))
        for z in range(L):
            out[step, z + odd * (L - 1 - 2 * z)] = u[7 + z]


def body(guesses, forcing, initial, kappa, velocity):
    count, times = lax.axis_size("space"), lax.axis_size("tm")
    facing = [(i, i + 1) for i in range(1, count - 1, 2)]
    facing += [(b, a) for a, b in facing]
    paired = [(i, i ^ 1) for i in range(count)]

    def from_outer(x):
        return lax.ppermute(x, "space", facing)

    def from_inner(x):
        return lax.ppermute(x, "space", paired)

    same = [(i, i) for i in range(count)]

    def move(x, intervals, moves=same):
        pairs = [(a * count + i, b * count + j) for a, b in intervals for i, j in moves]
        return lax.ppermute(x, ("tm", "space"), pairs)

    def hop(x, intervals, others=()):
        block, outer = move(x, [*intervals, *others]), move(x, intervals, facing)
        pair = lax.all_gather(block, "space", axis_index_groups=[[i, i + 1] for i in range(0, count, 2)])
        return block, outer, pair

    hbm = pl.BlockSpec(memory_space=pltpu.HBM)
    own, outer, inner, open_outer, open_inner = pl.pallas_call(
        pack_kernel,
        out_shape=[jax.ShapeDtypeStruct((n, NY, NX), jnp.float32) for n in (7 * L, FIRST, FIRST, OPEN, OPEN)],
        in_specs=[hbm] * 5,
        out_specs=[hbm] * 5,
        scratch_shapes=[
            VMEM((7, L, NY, NX), jnp.float32),
            *[VMEM((n, NY, NX), jnp.float32) for n in (7 * L, FIRST + OPEN, FIRST + OPEN)],
            pltpu.SemaphoreType.DMA((7,)),
            pltpu.SemaphoreType.DMA((21,)),
        ],
    )(guesses, forcing, kappa, velocity, initial)
    outer, inner = from_outer(outer), from_inner(inner)
    open_outer, open_inner = move(open_outer, [(0, 0)], facing), move(open_inner, [(0, 0)], paired)
    (own,) = call(settle_kernel, (7 * L,))(own)
    d, phi, fine = call(local_kernel, (L, L + 6, (7, L + 2 * FINE_HALO)), (L + 8, L + 14, L + 4))(
        own, outer, inner, open_outer, open_inner
    )
    (coef,) = call(coarse_kernel, ((7, L + 2 * COARSE_HALO),))(own, outer, inner)
    g = lax.all_gather(d, "tm", axis_index_groups=[[4 * a + b for b in range(4)] for a in range(times // 4)])
    slab_outer, slab_inner = call(slab_pack_kernel, (12, 12))(g)
    slab_outer, slab_inner = from_outer(slab_outer), from_inner(slab_inner)
    total, partial, prefix = call(slab_kernel, (L, L, L + 6), (L + 12,))(g, slab_outer, slab_inner, coef)

    def after(slab):
        return [(t, t + 4) for t in range(4 * slab, 4 * slab + 4)]

    one = hop(total, after(0))
    opening, send = call(chain1_kernel, (L, L), (3 * L,))(*one, total, partial, d, coef)
    (leaving,) = call(leave_kernel, (L + 6,))(phi, total)
    before = move(leaving, [(t, t + 1) for t in range(times - 1)])
    two = hop(send, after(1) + [(0, 4)], [(11, 12)])
    send, before = call(chain2_kernel, (L, L + 6), (3 * L,))(*two, total, partial, opening, coef, before)
    three = hop(send, after(2) + [(4, 8)])
    (out,) = call(finish_kernel, ((4, L),), (L + 14, L + 6))(
        *one, *two, *three, before, g, prefix, phi, own, outer, inner, open_outer, open_inner, coef, fine
    )
    return out


def solution(mesh):
    placed = (
        P("tm", "space", None, None),
        P("tm", "space", None, None),
        P("space", None, None),
        P("space", None, None),
        P(None, "space", None, None),
    )
    return jax.shard_map(
        body, mesh=mesh, in_specs=placed, out_specs=P("tm", "space", None, None), check_vma=False
    )
```

```python
import functools

import jax
import jax.numpy as jnp
from jax import lax
from jax.experimental import pallas as pl
from jax.experimental.pallas import tpu as pltpu
from jax.sharding import PartitionSpec as P


L = 8
NY, NX = 32, 128
STEP = 0.3
FINE_HALO = 6
COARSE_HALO = 7
SENT = (4, 6, COARSE_HALO)
COEFS = SENT[0] + SENT[1]
FIRST = COEFS + 4 * COARSE_HALO
OPEN = 7
VMEM = pltpu.VMEM


def call(kernel, outs, scratch=()):
    return pl.pallas_call(
        kernel,
        out_shape=[jax.ShapeDtypeStruct((n, NY, NX) if isinstance(n, int) else n + (NY, NX), jnp.float32) for n in outs],
        scratch_shapes=[VMEM((n, NY, NX), jnp.float32) for n in scratch],
        compiler_params=pltpu.CompilerParams(vmem_limit_bytes=40 << 20),
    )


def stencil(u, at, cur, prev, nxt, coef, k):
    return (
        coef[0, k] * nxt
        + coef[1, k] * prev
        + coef[2, k] * pltpu.roll(cur, NY - 1, 0)
        + coef[3, k] * pltpu.roll(cur, 1, 0)
        + coef[4, k] * pltpu.roll(cur, NX - 1, 1)
        + coef[5, k] * pltpu.roll(cur, 1, 1)
        + coef[6, k] * cur
    )


def sweep(u, base, coef, coef_base, lo, hi, after=None):
    prev, cur = u[lo - 1 + base], u[lo + base]
    for z in range(lo, hi):
        nxt = u[z + 1 + base]
        new = stencil(u, z, cur, prev, nxt, coef, z + coef_base)
        u[z + base] = new if after is None else after(z, cur, new)
        prev, cur = cur, nxt


def coarse_twice(u, base, coef, halo):
    sweep(u, base, coef, COARSE_HALO, 1 - halo, L + halo - 1)
    sweep(u, base, coef, COARSE_HALO, 2 - halo, L + halo - 2)


def ext(own, outer, inner, z, outer_at=0, inner_at=0, own_at=0):
    if z < 0:
        return outer[outer_at - 1 - z]
    if z >= L:
        return inner[inner_at + z - L]
    return own[own_at + z]


def write_coefs(out, index, diffuse, vz, vy, vx, h):
    row = lax.broadcasted_iota(jnp.int32, (NY, NX), 0)
    lane = lax.broadcasted_iota(jnp.int32, (NY, NX), 1)
    zero = jnp.zeros((NY, NX), jnp.float32)

    def pair(v):
        return h * (diffuse - jnp.minimum(v, 0.0)), h * (diffuse + jnp.maximum(v, 0.0))

    (above_z, below_z), (above_y, below_y), (above_x, below_x) = pair(vz), pair(vy), pair(vx)
    out[0, index] = above_z
    out[1, index] = below_z
    out[2, index] = jnp.where(row == NY - 1, zero, above_y)
    out[3, index] = jnp.where(row == 0, zero, below_y)
    out[4, index] = jnp.where(lane == NX - 1, zero, above_x)
    out[5, index] = jnp.where(lane == 0, zero, below_x)
    out[6, index] = 1.0 - (above_z + below_z + above_y + below_y + above_x + below_x)


def pack_kernel(
    guesses, forcing, kappa, velocity, initial, own, outer, inner, open_outer, open_inner, held, kept, low, high, sems, out_sems
):
    odd = lax.axis_index("space") % 2
    first = (lax.axis_index("tm") == 0).astype(jnp.float32)
    scale = (None, STEP, None, (1 - 2 * odd).astype(jnp.float32), None, None, first)
    sources = (guesses.at[0], forcing.at[0], kappa, velocity.at[0], velocity.at[1], velocity.at[2], initial)
    copies = [pltpu.make_async_copy(source, held.at[k], sems.at[k]) for k, source in enumerate(sources)]
    for copy in copies:
        copy.start()
    leaving, at = [], 0
    for field, copy in enumerate(copies):
        copy.wait()
        for z in range(L):
            value = held[field, z + odd * (L - 1 - 2 * z)]
            kept[field * L + z] = value if scale[field] is None else scale[field] * value
        count = SENT[min(field, 2)] if field < 6 else OPEN
        for i in range(count):
            low[at + i] = kept[field * L + i]
            high[at + i] = kept[field * L + L - 1 - i]
        spots, block = pl.ds(at, count), pl.ds(field * L, L)
        for k, (source, to) in enumerate((
            (low.at[spots], outer.at[spots] if field < 6 else open_outer),
            (high.at[spots], inner.at[spots] if field < 6 else open_inner),
            (kept.at[block], own.at[block]),
        )):
            leaving.append(pltpu.make_async_copy(source, to, out_sems.at[3 * field + k]))
            leaving[-1].start()
        at += count
    for copy in leaving:
        copy.wait()


def settle_kernel(held, own):
    for i in range(7 * L):
        own[i] = held[i]


def local_kernel(own, outer, inner, open_outer, open_inner, d, phi, coef, c, y, b):
    def get(field, z):
        if field == 6:
            return ext(own, open_outer, open_inner, z, 0, 0, 6 * L)
        at = (0, SENT[0], *range(COEFS, FIRST, COARSE_HALO))[field]
        return ext(own, outer, inner, z, at, at, field * L)

    for z in range(-FINE_HALO, L + FINE_HALO):
        vz = get(3, z)
        if not 0 <= z < L:
            vz = -vz
        write_coefs(coef, z + FINE_HALO, get(2, z), vz, get(4, z), get(5, z), STEP)
    opens = lax.axis_index("tm") == 0
    for z in range(-7, L + 7):
        y[z + 7] = get(6, z)
    for z in range(-4, L + 4):
        c[z + 4] = get(0, z)
    for step in range(4):
        halo = 6 - step
        if step == 0:

            @pl.when(opens)
            def _():
                sweep(y, 7, coef, FINE_HALO, -6, L + 6, lambda z, cur, new: new + get(1, z))

            @pl.when(jnp.logical_not(opens))
            def _():
                for z in range(-6, L + 6):
                    y[z + 7] = get(1, z)
        else:
            sweep(y, 7, coef, FINE_HALO, -halo, L + halo, lambda z, cur, new: new + get(1, z))
        halo = 3 - step
        sweep(c, 4, coef, FINE_HALO, -halo, L + halo)
    for z in range(-2, L + 2):
        b[z + 2] = y[z + 7] - get(0, z)
    for z in range(-3, L + 3):
        phi[z + 3] = y[z + 7]
    for halo in (1, 0):
        sweep(b, 2, coef, FINE_HALO, -halo, L + halo, lambda z, cur, new: 2.0 * new - cur)
    for z in range(L):
        d[z] = c[z + 4] + b[z + 2]


def coarse_kernel(own, outer, inner, coef):
    def get(k, z):
        at = COEFS + k * COARSE_HALO
        return ext(own, outer, inner, z, at, at, (2 + k) * L)

    for z in range(-COARSE_HALO, L + COARSE_HALO):
        vz = get(1, z)
        if not 0 <= z < L:
            vz = -vz
        write_coefs(coef, z + COARSE_HALO, get(0, z), vz, get(2, z), get(3, z), 2.0 * STEP)


def slab_pack_kernel(g, outer, inner):
    at = 0
    for k, count in enumerate((6, 4, 2)):
        for i in range(count):
            outer[at] = g[k, i]
            inner[at] = g[k, L - 1 - i]
            at += 1


def slab_kernel(g, outer, inner, coef, total, partial, prefix, v):
    place = lax.axis_index("tm") % 4
    for z in range(-6, L + 6):
        v[z + 6] = ext(g.at[0], outer, inner, z)

    def keep(wanted):
        @pl.when(place == wanted)
        def _():
            for z in range(-3, L + 3):
                prefix[z + 3] = v[z + 6]

    @pl.when(place < 2)
    def _():
        for z in range(L + 6):
            prefix[z] = jnp.zeros((NY, NX), jnp.float32)

    keep(2)
    coarse_twice(v, 6, coef, 6)
    for z in range(-4, L + 4):
        v[z + 6] += ext(g.at[1], outer, inner, z, 6, 6)
    keep(3)
    coarse_twice(v, 6, coef, 4)
    for z in range(-2, L + 2):
        v[z + 6] += ext(g.at[2], outer, inner, z, 10, 10)
    for z in range(L):
        partial[z] = v[z + 6]
    coarse_twice(v, 6, coef, 2)
    for z in range(L):
        total[z] = v[z + 6] + g[3, z]


def arrived(block, outer, pair):
    other = 1 - lax.axis_index("space") % 2
    return lambda z: outer[-1 - z] if z < 0 else pair[other, 2 * L - 1 - z] if z >= L else block[z]


def leave_kernel(phi, total, leaving):
    for i in range(L + 6):
        leaving[i] = phi[i]


def chain1_kernel(block, outer, pair, total, partial, d, coef, opening, send, u):
    here = lax.axis_index("tm") // 4 == 1
    get = arrived(block, outer, pair)

    @pl.when(here)
    def _():
        for z in range(-L, 2 * L):
            u[L + z] = get(z)
        for i in range(3):
            coarse_twice(u, L, coef, 8 - 2 * i)
        for z in range(L):
            opening[z] = u[L + z] + partial[z]
        coarse_twice(u, L, coef, 2)
        for z in range(L):
            send[z] = u[L + z] + total[z]

    @pl.when(jnp.logical_not(here))
    def _():
        for z in range(L):
            opening[z] = partial[z]
            send[z] = d[z]

    @pl.when(lax.axis_index("tm") // 4 == 0)
    def _():
        for z in range(L):
            send[z] = partial[z]


def chain2_kernel(block, outer, pair, total, partial, opening, coef, before, send, kept, u):
    for i in range(L + 6):
        kept[i] = before[i]
    here, place = lax.axis_index("tm") // 4 == 2, lax.axis_index("tm") % 4
    get = arrived(block, outer, pair)

    @pl.when(here)
    def _():
        for z in range(-L, 2 * L):
            u[L + z] = get(z)
        for i in range(3):
            coarse_twice(u, L, coef, 8 - 2 * i)

        @pl.when(place == 0)
        def _():
            for z in range(L):
                send[z] = u[L + z] + partial[z]

        @pl.when(place > 0)
        def _():
            coarse_twice(u, L, coef, 2)
            for z in range(L):
                send[z] = u[L + z] + total[z]

    @pl.when(jnp.logical_not(here))
    def _():
        for z in range(L):
            send[z] = opening[z]


def finish_kernel(b1, o1, p1, b2, o2, p2, b3, o3, p3, before, g, prefix, phi, own, outer, inner, open_outer, open_inner, coef, fine, out, u, w):
    t = lax.axis_index("tm")
    group, place = t // 4, t % 4
    odd = lax.axis_index("space") % 2

    def put(wanted, into, halo, get):
        @pl.when(wanted)
        def _():
            for z in range(-halo, L + halo):
                into[halo + z] = get(z)

    source = jnp.where(jnp.logical_and(place == 0, group > 0), jnp.minimum(group + 1, 3), group)
    put(source == 0, u, 7, lambda z: jnp.zeros((NY, NX), jnp.float32))
    put(source == 1, u, 7, arrived(b1, o1, p1))
    put(source == 2, u, 7, arrived(b2, o2, p2))
    put(source == 3, u, 7, arrived(b3, o3, p3))
    @pl.when(place == 3)
    def _():
        sweep(u, 7, coef, COARSE_HALO, -6, L + 6)
        sweep(u, 7, coef, COARSE_HALO, -5, L + 5)

    @pl.when(place >= 2)
    def _():
        sweep(u, 7, coef, COARSE_HALO, -4, L + 4)
        sweep(u, 7, coef, COARSE_HALO, -3, L + 3)

    for z in range(-3, L + 3):
        w[3 + z] = u[7 + z] + prefix[3 + z]

    @pl.when(t == 0)
    def _():
        for z in range(-3, L + 3):
            u[7 + z] = w[3 + z] + ext(own, open_outer, open_inner, z, 0, 0, 6 * L)

    @pl.when(t > 0)
    def _():
        for z in range(-3, L + 3):
            u[7 + z] = w[3 + z] + before[3 + z]

    coarse_twice(w, 3, coef, 2)

    def last(wanted, get):
        @pl.when(wanted)
        def _():
            for z in range(L):
                out[3, z + odd * (L - 1 - 2 * z)] = get(z) + phi[3 + z]

    last(place > 0, lambda z: w[3 + z] + g[place - 1, z])
    last(t == 0, lambda z: w[3 + z])
    last(t == 4, lambda z: b1[z])
    last(t == 8, lambda z: b2[z])
    last(t == 12, lambda z: w[3 + z] + b2[z])
    at = SENT[0]
    for step in range(3):
        halo = 2 - step
        sweep(u, 7, fine, FINE_HALO, -halo, L + halo,
              lambda z, cur, new: new + ext(own, outer, inner, z, at, at, L))
        for z in range(L):
            out[step, z + odd * (L - 1 - 2 * z)] = u[7 + z]


def body(guesses, forcing, initial, kappa, velocity):
    count, times = lax.axis_size("space"), lax.axis_size("tm")
    facing = [(i, i + 1) for i in range(1, count - 1, 2)]
    facing += [(b, a) for a, b in facing]
    paired = [(i, i ^ 1) for i in range(count)]

    def from_outer(x):
        return lax.ppermute(x, "space", facing)

    def from_inner(x):
        return lax.ppermute(x, "space", paired)

    same = [(i, i) for i in range(count)]

    def move(x, intervals, moves=same):
        pairs = [(a * count + i, b * count + j) for a, b in intervals for i, j in moves]
        return lax.ppermute(x, ("tm", "space"), pairs)

    def hop(x, intervals, others=()):
        block, outer = move(x, [*intervals, *others]), move(x, intervals, facing)
        pair = lax.all_gather(block, "space", axis_index_groups=[[i, i + 1] for i in range(0, count, 2)])
        return block, outer, pair

    hbm = pl.BlockSpec(memory_space=pltpu.HBM)
    own, outer, inner, open_outer, open_inner = pl.pallas_call(
        pack_kernel,
        out_shape=[jax.ShapeDtypeStruct((n, NY, NX), jnp.float32) for n in (7 * L, FIRST, FIRST, OPEN, OPEN)],
        in_specs=[hbm] * 5,
        out_specs=[hbm] * 5,
        scratch_shapes=[
            VMEM((7, L, NY, NX), jnp.float32),
            *[VMEM((n, NY, NX), jnp.float32) for n in (7 * L, FIRST + OPEN, FIRST + OPEN)],
            pltpu.SemaphoreType.DMA((7,)),
            pltpu.SemaphoreType.DMA((21,)),
        ],
    )(guesses, forcing, kappa, velocity, initial)
    outer, inner = from_outer(outer), from_inner(inner)
    open_outer, open_inner = move(open_outer, [(0, 0)], facing), move(open_inner, [(0, 0)], paired)
    (own,) = call(settle_kernel, (7 * L,))(own)
    d, phi, fine = call(local_kernel, (L, L + 6, (7, L + 2 * FINE_HALO)), (L + 8, L + 14, L + 4))(
        own, outer, inner, open_outer, open_inner
    )
    (coef,) = call(coarse_kernel, ((7, L + 2 * COARSE_HALO),))(own, outer, inner)
    g = lax.all_gather(d, "tm", axis_index_groups=[[4 * a + b for b in range(4)] for a in range(times // 4)])
    slab_outer, slab_inner = call(slab_pack_kernel, (12, 12))(g)
    slab_outer, slab_inner = from_outer(slab_outer), from_inner(slab_inner)
    total, partial, prefix = call(slab_kernel, (L, L, L + 6), (L + 12,))(g, slab_outer, slab_inner, coef)

    def after(slab):
        return [(t, t + 4) for t in range(4 * slab, 4 * slab + 4)]

    one = hop(total, after(0))
    opening, send = call(chain1_kernel, (L, L), (3 * L,))(*one, total, partial, d, coef)
    (leaving,) = call(leave_kernel, (L + 6,))(phi, total)
    before = move(leaving, [(t, t + 1) for t in range(times - 1)])
    two = hop(send, after(1) + [(0, 4)], [(11, 12)])
    send, before = call(chain2_kernel, (L, L + 6), (3 * L,))(*two, total, partial, opening, coef, before)
    three = hop(send, after(2) + [(4, 8)])
    (out,) = call(finish_kernel, ((4, L),), (L + 14, L + 6))(
        *one, *two, *three, before, g, prefix, phi, own, outer, inner, open_outer, open_inner, coef, fine
    )
    return out


def solution(mesh):
    placed = (
        P("tm", "space", None, None),
        P("tm", "space", None, None),
        P("space", None, None),
        P("space", None, None),
        P(None, "space", None, None),
    )
    return jax.shard_map(
        body, mesh=mesh, in_specs=placed, out_specs=P("tm", "space", None, None), check_vma=False
    )
```
